32 devices in a mesh: layer: 2 (over y), latent: 16 (over z, x, core).
Axes of the slice: x: 2, y: 2, z: 4, core: 2. Of those that a mesh axis runs over, the one named last changes fastest.
Arguments:
- acts: bfloat16 [1280, 4608], P(None, 'layer'), may hold values from -6 to 6
- enc_weight: bfloat16 [4608, 32768], P('layer', 'latent'), may hold values from -0.09375 to 0.09375
- enc_bias: float32 [32768], P('latent'), may hold values from -3 to 3
- dec_weight: bfloat16 [32768, 4608], P('latent', 'layer'), may hold values from -0.3314563 to 0.3314563, as said below
- dec_bias: float32 [4608], P('layer'), may hold values from -2 to 2
Outputs:
- grad_enc: float32 [4608, 32768], P('layer', 'latent')
- grad_enc_bias: float32 [32768], P('latent')
- grad_dec: float32 [32768, 4608], P('latent', 'layer')
- grad_dec_bias: float32 [4608], P('layer')
The draws below stay inside these ranges and needn't reach their ends.
Inputs may be any that keep to these rules, and one draw needn't show every extreme that they name: `dec_weight`: decoder entries lie within 60 / sqrt(32768) of zero.
All inputs are finite; a program needn't handle non-finite values.
Results may differ from the reference program's by a relative error of at most 0.0045.
Values may be sent and summed in bfloat16 or wider, within the bound.
A program may use at most 192 MiB of HBM per device.

```python
import math
import jax
import jax.numpy as jnp
from jax import lax

D = 2304
LAYERS = 2
LATENTS = 32768
ROWS = 1280
FEAT = 4608


def draw_dec_weight(key, part):
    key = jax.random.fold_in(key, 11)
    key_rows, key_base = jax.random.split(key, 2)
    width = LAYERS * D
    row_scale = jnp.exp(jax.random.uniform(key_rows, (LATENTS, 1), jnp.float32) * math.log(10.0))
    position = jnp.arange(width).astype(jnp.float32) / (width - 1)
    col_scale = jnp.exp(position * math.log(3.0))[None, :]
    base = jnp.clip(jax.random.normal(key_base, (LATENTS, width), jnp.float32), -6.0, 6.0)
    values = base * row_scale * col_scale / (3.0 * math.sqrt(LATENTS))
    return values.astype(jnp.bfloat16)


def levels(stream_key, shape, cuts, least, largest):
    loudness = 1.0
    for dim, parts in cuts:
        steps = jax.random.uniform(jax.random.fold_in(jax.random.fold_in(stream_key, 6), dim), (parts,), jnp.float32, least / len(cuts), largest / len(cuts))
        loudness = loudness * jnp.repeat(jnp.exp(steps), shape[dim] // parts).reshape((-1,) + (1,) * (len(shape) - 1 - dim))
    return loudness


def bell_draw(rng, extent, scale, limit, cuts=(), dtype=jnp.bfloat16):
    values = jax.random.normal(rng, extent, jnp.float32) * scale
    if len(cuts) > 0:
        values = levels(rng, extent, cuts, -0.22, 0.18) * values
    return jnp.clip(values, min=-limit, max=limit).astype(dtype)


def setup_inputs(seed: int = 0) -> dict:
    arg_keys = jax.random.split(jax.random.key(seed), 6)
    return {
        "acts": bell_draw(arg_keys[0], (ROWS, FEAT), 1.0, 6.0, ((1, 2),)),
        "enc_weight": bell_draw(arg_keys[1], (FEAT, LATENTS), FEAT ** -0.5, 0.09375, ((0, 2), (1, 16))),
        "enc_bias": bell_draw(arg_keys[2], (LATENTS,), 0.5, 3.0, ((0, 16),), jnp.float32),
        "dec_weight": draw_dec_weight(jax.random.fold_in(arg_keys[5], 71), 0),
        "dec_bias": bell_draw(arg_keys[4], (FEAT,), 0.3, 2.0, ((0, 2),), jnp.float32),
    }


def reference(acts, enc_weight, enc_bias, dec_weight, dec_bias):
    scale = 1.0 / jnp.sqrt(jnp.float32(ROWS))
    sparsity = 1.0
    pre = jnp.dot(acts, enc_weight, preferred_element_type=jnp.float32) + enc_bias
    codes = jax.nn.softplus(pre).astype(jnp.bfloat16)
    slope = jax.nn.sigmoid(pre)
    dec_f = dec_weight.astype(jnp.float32)
    norms = jnp.sqrt(lax.optimization_barrier(jnp.sum(dec_f * dec_f, axis=1)) + 1e-06)
    recon = jnp.dot(codes, dec_weight, preferred_element_type=jnp.float32) + dec_bias
    err_grad = (2.0 * scale * (recon - acts.astype(jnp.float32))).astype(jnp.bfloat16)
    grad_dec_bias = lax.optimization_barrier(jnp.sum(err_grad.astype(jnp.float32), axis=0))
    column = lax.optimization_barrier(jnp.sum(codes.astype(jnp.float32), axis=0))
    grad_dec = lax.dot_general(codes, err_grad, (((0,), (0,)), ((), ())), preferred_element_type=jnp.float32)
    grad_dec = grad_dec + (sparsity * scale * column / norms)[:, None] * dec_f
    back = lax.dot_general(err_grad, dec_weight, (((1,), (1,)), ((), ())), preferred_element_type=jnp.float32)
    back = back + sparsity * scale * norms
    delta = (back * slope).astype(jnp.bfloat16)
    grad_enc = lax.dot_general(acts, delta, (((0,), (0,)), ((), ())), preferred_element_type=jnp.float32)
    grad_enc_bias = lax.optimization_barrier(jnp.sum(delta.astype(jnp.float32), axis=0))
    return (grad_enc, grad_enc_bias, grad_dec, grad_dec_bias)
```

```python
import jax
import jax.numpy as jnp
from jax import lax
from jax.sharding import PartitionSpec as P

LOCAL = 4


def split_rows(rows):
    for parts in (5, 4, 2):
        if rows % (parts * 16) == 0:
            return parts
    return 1


def rows_of(array, start, count):
    return lax.dynamic_slice_in_dim(array, start, count, axis=0)


def make_per_device(n_layer, n_latent):
    depth = n_latent // LOCAL

    def swap(array, bit):
        return lax.ppermute(array, "latent", [(i, i ^ bit) for i in range(n_latent)])

    def shift(array, step):
        pairs = [(i, (i + step * LOCAL) % n_latent) for i in range(n_latent)]
        return lax.ppermute(array, "latent", pairs)

    def other_layer(array):
        return lax.ppermute(array, "layer", [(0, 1), (1, 0)])

    def over_layer(array, other):
        own = array.astype(jnp.float32)
        if n_layer == 2:
            return own + other.astype(jnp.float32)
        return lax.psum(own, "layer")

    groups = [[z * LOCAL + c for z in range(depth)] for c in range(LOCAL)]

    def per_device(acts, enc_weight, enc_bias, dec_weight, dec_bias):
        rows = acts.shape[0]
        parts = split_rows(rows)
        part = rows // parts
        scale = 1.0 / jnp.sqrt(jnp.float32(rows))
        sparsity = 1.0
        index = lax.axis_index("latent")
        z, x, core = index // LOCAL, (index // 2) % 2, index % 2

        done = []

        def send_layer(array):
            if n_layer != 2:
                return array, None
            if len(done) >= 2:
                array, earlier = lax.optimization_barrier((array, done[-2]))
                del earlier
            other = other_layer(array)
            done.append(other)
            return array, other

        dec_f = dec_weight.astype(jnp.float32)
        squares = jnp.sum(dec_f * dec_f, axis=1)
        squares = over_layer(squares, other_layer(squares) if n_layer == 2 else None)
        norms = jnp.sqrt(squares + 1e-06)

        def encode(k):
            block = acts[k * part : (k + 1) * part]
            own = jnp.dot(block, enc_weight, preferred_element_type=jnp.float32)
            return send_layer(own.astype(jnp.float16))

        def reduce_latent(partial):
            half, quarter = part // 2, part // 4
            piece = quarter // depth
            got = swap(rows_of(partial, (1 - core) * half, half), 1)
            held = rows_of(partial, core * half, half) + got
            got = swap(rows_of(held, (1 - x) * quarter, quarter).astype(jnp.bfloat16), 2)
            held = rows_of(held, x * quarter, quarter) + got.astype(jnp.float32)
            if depth > 4:
                return lax.psum_scatter(
                    held, "latent", scatter_dimension=0, axis_index_groups=groups, tiled=True
                )
            total = rows_of(held, z * piece, piece)
            for step in range(1, depth):
                target = (z + step) % depth
                got = shift(rows_of(held, target * piece, piece).astype(jnp.bfloat16), step)
                total = total + got.astype(jnp.float32)
            return total

        def gather_latent(own):
            piece = own.shape[0]
            if depth > 4:
                held = lax.all_gather(own, "latent", axis_index_groups=groups, tiled=True)
            else:
                held = jnp.zeros((piece * depth, own.shape[1]), own.dtype)
                held = lax.dynamic_update_slice_in_dim(held, own, z * piece, axis=0)
                for step in range(1, depth):
                    source = (z - step + depth) % depth
                    held = lax.dynamic_update_slice_in_dim(
                        held, shift(own, step), source * piece, axis=0
                    )
            for bit, place in ((2, x), (1, core)):
                got = swap(held, bit)
                low = jnp.where(place == 0, held, got)
                high = jnp.where(place == 0, got, held)
                held = jnp.concatenate([low, high], axis=0)
            return held

        def decode(k, own, other):
            pre = over_layer(own, other) + enc_bias
            codes = jax.nn.softplus(pre).astype(jnp.bfloat16)
            partial = jnp.dot(codes, dec_weight, preferred_element_type=jnp.float32)
            total = reduce_latent(partial)
            piece = total.shape[0]
            start = k * part + core * (part // 2) + x * (part // 4) + z * piece
            mine = rows_of(acts, start, piece).astype(jnp.float32)
            err = (2.0 * scale * (total + dec_bias - mine)).astype(jnp.bfloat16)
            return codes, gather_latent(err)

        def back_of(err):
            own = lax.dot_general(
                err, dec_weight, (((1,), (1,)), ((), ())), preferred_element_type=jnp.float32
            )
            return send_layer(own.astype(jnp.bfloat16))

        pres = [encode(k) for k in range(parts)]
        codes, errs = [], []
        for k in range(parts):
            c, e = decode(k, *pres[k])
            codes.append(c)
            errs.append(e)
        backs = [back_of(e) for e in errs]

        codes = jnp.concatenate(codes, axis=0)
        err_grad = jnp.concatenate(errs, axis=0)
        grad_dec_bias = jnp.sum(err_grad.astype(jnp.float32), axis=0)
        column = jnp.sum(codes.astype(jnp.float32), axis=0)
        grad_dec = lax.dot_general(
            codes, err_grad, (((0,), (0,)), ((), ())), preferred_element_type=jnp.float32
        )
        grad_dec = grad_dec + (sparsity * scale * column / norms)[:, None] * dec_f

        deltas = []
        for k in range(parts):
            slope = jax.nn.sigmoid(over_layer(*pres[k]) + enc_bias)
            back = over_layer(*backs[k]) + sparsity * scale * norms
            deltas.append((back * slope).astype(jnp.bfloat16))
        delta = jnp.concatenate(deltas, axis=0)
        grad_enc = lax.dot_general(
            acts, delta, (((0,), (0,)), ((), ())), preferred_element_type=jnp.float32
        )
        grad_enc_bias = jnp.sum(delta.astype(jnp.float32), axis=0)
        return (grad_enc, grad_enc_bias, grad_dec, grad_dec_bias)

    return per_device


def solution(mesh):
    return jax.shard_map(
        make_per_device(mesh.shape["layer"], mesh.shape["latent"]),
        mesh=mesh,
        in_specs=(
            P(None, "layer"),
            P("layer", "latent"),
            P("latent"),
            P("latent", "layer"),
            P("layer"),
        ),
        out_specs=(P("layer", "latent"), P("latent"), P("latent", "layer"), P("layer")),
        check_vma=False,
    )
```

```python
import functools

import jax
import jax.numpy as jnp
import numpy as np
from jax import lax
from jax.experimental import pallas as pl
from jax.experimental.pallas import tpu as pltpu
from jax.sharding import PartitionSpec as P

OVER_ROWS = (((0,), (0,)), ((), ()))
OVER_COLUMNS = (((1,), (1,)), ((), ()))
WIRE = jnp.bfloat16
PARAMS = pltpu.CompilerParams(vmem_limit_bytes=44 * 2**20)


def split_rows(rows):
    for parts in (5, 4, 2):
        if rows % (parts * 64) == 0:
            return parts
    return 1


def block_of(size, least=256):
    return least if size % least == 0 else size


def softplus(x):
    return jnp.maximum(x, 0.0) + jnp.log1p(jnp.exp(-jnp.abs(x)))


def delta_of(own_back, other_back, own_pre, other_pre, bias, penalty):
    pre = own_pre.astype(jnp.float32) + other_pre.astype(jnp.float32) + bias
    back = own_back.astype(jnp.float32) + other_back.astype(jnp.float32) + penalty
    return (back * jax.nn.sigmoid(pre)).astype(jnp.bfloat16)


def slot_kernel(tasks, n_in, *refs):
    ins, outs = list(refs[:n_in]), list(refs[n_in:])
    if "send" in tasks:
        send_sem, recv_sem = outs.pop(-2), outs.pop(-1)
        payload, received = ins.pop(0), outs.pop(0)
        partner = {"layer": 1 - lax.axis_index("layer")}
        exchange = pltpu.make_async_remote_copy(
            src_ref=payload,
            dst_ref=received,
            send_sem=send_sem,
            recv_sem=recv_sem,
            device_id=partner,
            device_id_type=pl.DeviceIdType.MESH,
        )

        @pl.when(pl.program_id(0) == 0)
        def _():
            barrier = pltpu.get_barrier_semaphore()
            pl.semaphore_signal(
                barrier, inc=1, device_id=partner, device_id_type=pl.DeviceIdType.MESH
            )
            pl.semaphore_wait(barrier, 1)
            exchange.start()

    def take(count):
        taken = ins[:count]
        del ins[:count]
        return taken

    if "encode" in tasks:
        acts, weight = take(2)
        own = jnp.dot(acts[...], weight[...], preferred_element_type=jnp.float32)
        outs.pop(0)[...] = own.astype(WIRE)
    if "recon" in tasks or "back" in tasks:
        (dec,) = take(1)
    if "recon" in tasks:
        own_pre, other_pre, bias = take(3)
        pre = own_pre[...].astype(jnp.float32) + other_pre[...].astype(jnp.float32) + bias[...]
        codes = softplus(pre).astype(jnp.bfloat16)
        outs.pop(0)[...] = codes
        total = outs.pop(0)
        product = jnp.dot(codes, dec[...], preferred_element_type=jnp.float32)

        @pl.when(pl.program_id(0) == 0)
        def _():
            total[...] = product

        @pl.when(pl.program_id(0) > 0)
        def _():
            total[...] += product

    if "back" in tasks:
        (err,) = take(1)
        own = lax.dot_general(
            err[...], dec[...], OVER_COLUMNS, preferred_element_type=jnp.float32
        )
        outs.pop(0)[...] = own.astype(WIRE)
    if "delta" in tasks:
        values = [r[...] for r in take(6)]
        outs.pop(0)[...] = delta_of(*values)
    if "send" in tasks:

        @pl.when(pl.program_id(0) == pl.num_programs(0) - 1)
        def _():
            exchange.wait()


def run_slot(tasks, slot=0):
    if "encode" in tasks:
        part, latents = tasks["encode"][0].shape[0], tasks["encode"][1].shape[1]
    elif "recon" in tasks:
        part, latents = tasks["recon"][0].shape
    elif "back" in tasks:
        part, latents = tasks["back"][0].shape[0], tasks["dec"].shape[0]
    else:
        part, latents = tasks["delta"][0].shape
    width = tasks["dec"].shape[1]
    block = block_of(latents, 512)
    tile = pl.BlockSpec((part, block), lambda j: (0, j))
    line = pl.BlockSpec((1, block), lambda j: (0, j))
    whole = pl.BlockSpec((part, width), lambda j: (0, 0))
    operands, in_specs, shapes, out_specs, names = [], [], [], [], []
    flops = 0
    if "send" in tasks:
        operands.append(tasks["send"])
        in_specs.append(pl.BlockSpec(memory_space=pl.ANY))
        shapes.append(jax.ShapeDtypeStruct(tasks["send"].shape, tasks["send"].dtype))
        out_specs.append(pl.BlockSpec(memory_space=pl.ANY))
        names.append("received")
    if "encode" in tasks:
        operands += tasks["encode"]
        in_specs += [whole, pl.BlockSpec((width, block), lambda j: (0, j))]
        shapes.append(jax.ShapeDtypeStruct((part, latents), WIRE))
        out_specs.append(tile)
        names.append("encode")
        flops += 2 * part * width * latents
    if "recon" in tasks or "back" in tasks:
        operands.append(tasks["dec"])
        in_specs.append(pl.BlockSpec((block, width), lambda j: (j, 0)))
    if "recon" in tasks:
        operands += tasks["recon"]
        in_specs += [tile, tile, line]
        shapes.append(jax.ShapeDtypeStruct((part, latents), jnp.bfloat16))
        shapes.append(jax.ShapeDtypeStruct((part, width), jnp.float32))
        out_specs += [tile, whole]
        names += ["codes", "partial"]
        flops += 2 * part * width * latents
    if "back" in tasks:
        operands += tasks["back"]
        in_specs.append(whole)
        shapes.append(jax.ShapeDtypeStruct((part, latents), WIRE))
        out_specs.append(tile)
        names.append("back")
        flops += 2 * part * width * latents
    if "delta" in tasks:
        operands += tasks["delta"]
        in_specs += [tile, tile, tile, tile, line, line]
        shapes.append(jax.ShapeDtypeStruct((part, latents), jnp.bfloat16))
        out_specs.append(tile)
        names.append("delta")
    outs = pl.pallas_call(
        functools.partial(slot_kernel, tuple(tasks), len(operands)),
        grid=(latents // block,),
        out_shape=tuple(shapes),
        in_specs=in_specs,
        out_specs=tuple(out_specs),
        scratch_shapes=[pltpu.SemaphoreType.DMA] * 2 if "send" in tasks else [],
        compiler_params=pltpu.CompilerParams(
            vmem_limit_bytes=44 * 2**20, collective_id=slot, has_side_effects=True
        )
        if "send" in tasks
        else PARAMS,
        cost_estimate=pl.CostEstimate(
            flops=flops, bytes_accessed=4 * width * latents, transcendentals=2 * part * latents
        ),
    )(*operands)
    return dict(zip(names, outs))


def error_kernel(factor, total_ref, bias_ref, acts_ref, out_ref):
    err = factor * (total_ref[...] + bias_ref[...] - acts_ref[...].astype(jnp.float32))
    out_ref[...] = err.astype(jnp.bfloat16)


def error_of(factor, total, bias, acts):
    return pl.pallas_call(
        functools.partial(error_kernel, factor),
        out_shape=jax.ShapeDtypeStruct(total.shape, jnp.bfloat16),
    )(total, bias, acts)


def grad_dec_kernel(parts, *refs):
    codes, errs = refs[:parts], refs[parts : 2 * parts]
    coef_ref, dec_ref, out_ref = refs[2 * parts :]
    total = coef_ref[...] * dec_ref[...].astype(jnp.float32)
    code = jnp.concatenate([c[...] for c in codes], axis=0)
    err = jnp.concatenate([e[...] for e in errs], axis=0)
    out_ref[...] = total + lax.dot_general(
        code, err, OVER_ROWS, preferred_element_type=jnp.float32
    )


def grad_dec_of(codes, errs, coef, dec):
    part, latents = codes[0].shape
    width = errs[0].shape[1]
    block = block_of(latents)
    parts = len(codes)
    return pl.pallas_call(
        functools.partial(grad_dec_kernel, parts),
        grid=(latents // block,),
        out_shape=jax.ShapeDtypeStruct((latents, width), jnp.float32),
        in_specs=[pl.BlockSpec((part, block), lambda i: (0, i))] * parts
        + [pl.BlockSpec((part, width), lambda i: (0, 0))] * parts
        + [
            pl.BlockSpec((block, 1), lambda i: (i, 0)),
            pl.BlockSpec((block, width), lambda i: (i, 0)),
        ],
        out_specs=pl.BlockSpec((block, width), lambda i: (i, 0)),
        compiler_params=PARAMS,
        cost_estimate=pl.CostEstimate(
            flops=2 * parts * part * latents * width,
            bytes_accessed=latents * width * 6,
            transcendentals=0,
        ),
    )(*codes, *errs, coef, dec)


def grad_enc_kernel(parts, *refs):
    acts_ref, deltas = refs[0], refs[1 : parts + 1]
    out_ref, bias_ref = refs[parts + 1 :]

    @pl.when(pl.program_id(0) == 0)
    def _():
        total = jnp.zeros_like(bias_ref)
        for d in deltas:
            total += jnp.sum(d[...].astype(jnp.float32), axis=0, keepdims=True)
        bias_ref[...] = total

    delta = jnp.concatenate([d[...] for d in deltas], axis=0)
    out_ref[...] = lax.dot_general(
        acts_ref[...], delta, OVER_ROWS, preferred_element_type=jnp.float32
    )


def grad_enc_of(acts, deltas):
    rows, width = acts.shape
    part, latents = deltas[0].shape
    parts = len(deltas)
    block = block_of(width)
    return pl.pallas_call(
        functools.partial(grad_enc_kernel, parts),
        grid=(width // block,),
        out_shape=(
            jax.ShapeDtypeStruct((width, latents), jnp.float32),
            jax.ShapeDtypeStruct((1, latents), jnp.float32),
        ),
        in_specs=[pl.BlockSpec((rows, block), lambda i: (0, i))]
        + [pl.BlockSpec((part, latents), lambda i: (0, 0))] * parts,
        out_specs=(
            pl.BlockSpec((block, latents), lambda i: (i, 0)),
            pl.BlockSpec((1, latents), lambda i: (0, 0)),
        ),
        compiler_params=PARAMS,
        cost_estimate=pl.CostEstimate(
            flops=2 * rows * latents * width,
            bytes_accessed=latents * width * 4,
            transcendentals=0,
        ),
    )(acts, *deltas)


def make_per_device(n_layer, n_latent):
    def other_layer(array):
        if n_layer == 2:
            return lax.ppermute(array, "layer", [(0, 1), (1, 0)])
        wide = array.astype(jnp.float32)
        return lax.psum(wide, "layer") - wide

    def per_device(acts, enc_weight, enc_bias, dec_weight, dec_bias):
        rows = acts.shape[0]
        n = split_rows(rows)
        part = rows // n
        piece = part // n_latent
        scale = 1.0 / jnp.sqrt(jnp.float32(rows))
        factor = float(np.float32(2.0) * (np.float32(1.0) / np.sqrt(np.float32(rows))))
        sparsity = 1.0
        index = lax.axis_index("latent")
        bias = enc_bias[None, :]

        def after(array, earlier):
            return lax.optimization_barrier((array, earlier))[0]

        def acts_of(k):
            return acts[k * part : (k + 1) * part]

        dec_f = dec_weight.astype(jnp.float32)
        squares = jnp.sum(dec_f * dec_f, axis=1)
        norms = jnp.sqrt(squares + other_layer(squares) + 1e-06)
        penalty = (sparsity * scale * norms)[None, :]

        own_pre, other_pre, codes, partials, scattered, errs = {}, {}, {}, {}, {}, {}
        own_back, other_back, deltas = {}, {}, {}
        own_pre[0] = run_slot({"encode": (acts_of(0), enc_weight), "dec": dec_weight})["encode"]

        for s in range(2 * n - 1):
            payload = own_pre[s] if s < n else own_back[s - n]
            if 0 <= s - 3 < n:
                total = after(scattered[s - 3], payload)
                start = (s - 3) * part + index * piece
                mine = lax.dynamic_slice_in_dim(acts, start, piece, axis=0)
                err = error_of(factor, total, dec_bias[None, :], mine)
                errs[s - 3] = lax.all_gather(err, "latent", tiled=True)
            tasks = {"dec": dec_weight}
            if n_layer == 2:
                tasks["send"] = payload
            if s + 1 < n:
                tasks["encode"] = (after(acts_of(s + 1), payload), enc_weight)
            if 0 <= s - 1 < n:
                tasks["recon"] = (own_pre[s - 1], after(other_pre[s - 1], payload), bias)
            if 0 <= s - (n - 1) < n:
                tasks["back"] = (after(errs[s - (n - 1)], payload),)
            if 0 <= s - n - 1:
                k = s - n - 1
                tasks["delta"] = (
                    own_back[k], after(other_back[k], payload), own_pre[k], other_pre[k], bias, penalty
                )
            outs = run_slot(tasks, s)
            received = outs["received"] if n_layer == 2 else other_layer(payload)
            if s < n:
                other_pre[s] = received
            else:
                other_back[s - n] = received
            if "encode" in outs:
                own_pre[s + 1] = outs["encode"]
            if "partial" in outs:
                codes[s - 1], partials[s - 1] = outs["codes"], outs["partial"]
                scattered[s - 1] = lax.psum_scatter(
                    outs["partial"], "latent", scatter_dimension=0, tiled=True
                )
            if "back" in outs:
                own_back[s - (n - 1)] = outs["back"]
            if "delta" in outs:
                deltas[s - n - 1] = outs["delta"]

        payload = own_back[n - 1]
        other_back[n - 1] = other_layer(payload)
        column = sum(jnp.sum(codes[k].astype(jnp.float32), axis=0) for k in range(n))
        grad_dec_bias = sum(jnp.sum(errs[k].astype(jnp.float32), axis=0) for k in range(n))
        coef = after((sparsity * scale * column / norms)[:, None], payload)
        grad_dec = grad_dec_of(
            [codes[k] for k in range(n)], [errs[k] for k in range(n)], coef, dec_weight
        )
        other_back[n - 1] = after(other_back[n - 1], grad_dec)
        for k in range(n):
            if k not in deltas:
                tasks = {"dec": dec_weight}
                tasks["delta"] = (
                    own_back[k], other_back[k], own_pre[k], other_pre[k], bias, penalty
                )
                deltas[k] = run_slot(tasks)["delta"]
        grad_enc, grad_enc_bias = grad_enc_of(acts, [deltas[k] for k in range(n)])
        return (grad_enc, grad_enc_bias[0], grad_dec, grad_dec_bias)

    return per_device


def solution(mesh):
    return jax.shard_map(
        make_per_device(mesh.shape["layer"], mesh.shape["latent"]),
        mesh=mesh,
        in_specs=(
            P(None, "layer"),
            P("layer", "latent"),
            P("latent"),
            P("latent", "layer"),
            P("layer"),
        ),
        out_specs=(P("layer", "latent"), P("latent"), P("latent", "layer"), P("layer")),
        check_vma=False,
    )
```

```python
import functools

import jax
import jax.numpy as jnp
from jax import lax
from jax.experimental import pallas as pl
from jax.experimental.pallas import tpu as pltpu
from jax.sharding import PartitionSpec as P

LOCAL = 4


OVER_ROWS = (((0,), (0,)), ((), ()))
PARAMS = pltpu.CompilerParams(vmem_limit_bytes=44 * 2**20)


def block_of(size, least=256):
    return least if size % least == 0 else size


def split_rows(rows):
    for parts in (5, 4, 2):
        if rows % (parts * 16) == 0:
            return parts
    return 1


def rows_of(array, start, count):
    return lax.dynamic_slice_in_dim(array, start, count, axis=0)


def grad_dec_kernel(parts, *refs):
    codes, errs = refs[:parts], refs[parts : 2 * parts]
    coef_ref, dec_ref, out_ref = refs[2 * parts :]
    total = coef_ref[...] * dec_ref[...].astype(jnp.float32)
    code = jnp.concatenate([c[...] for c in codes], axis=0)
    err = jnp.concatenate([e[...] for e in errs], axis=0)
    out_ref[...] = total + lax.dot_general(
        code, err, OVER_ROWS, preferred_element_type=jnp.float32
    )


def grad_dec_of(codes, errs, coef, dec):
    part, latents = codes[0].shape
    width = errs[0].shape[1]
    block = block_of(latents)
    parts = len(codes)
    return pl.pallas_call(
        functools.partial(grad_dec_kernel, parts),
        grid=(latents // block,),
        out_shape=jax.ShapeDtypeStruct((latents, width), jnp.float32),
        in_specs=[pl.BlockSpec((part, block), lambda i: (0, i))] * parts
        + [pl.BlockSpec((part, width), lambda i: (0, 0))] * parts
        + [
            pl.BlockSpec((block, 1), lambda i: (i, 0)),
            pl.BlockSpec((block, width), lambda i: (i, 0)),
        ],
        out_specs=pl.BlockSpec((block, width), lambda i: (i, 0)),
        compiler_params=PARAMS,
        cost_estimate=pl.CostEstimate(
            flops=2 * parts * part * latents * width,
            bytes_accessed=latents * width * 6,
            transcendentals=0,
        ),
    )(*codes, *errs, coef, dec)


def grad_enc_kernel(parts, *refs):
    acts_ref, deltas = refs[0], refs[1 : parts + 1]
    out_ref, bias_ref = refs[parts + 1 :]

    @pl.when(pl.program_id(0) == 0)
    def _():
        total = jnp.zeros_like(bias_ref)
        for d in deltas:
            total += jnp.sum(d[...].astype(jnp.float32), axis=0, keepdims=True)
        bias_ref[...] = total

    delta = jnp.concatenate([d[...] for d in deltas], axis=0)
    out_ref[...] = lax.dot_general(
        acts_ref[...], delta, OVER_ROWS, preferred_element_type=jnp.float32
    )


def grad_enc_of(acts, deltas):
    rows, width = acts.shape
    part, latents = deltas[0].shape
    parts = len(deltas)
    block = block_of(width)
    return pl.pallas_call(
        functools.partial(grad_enc_kernel, parts),
        grid=(width // block,),
        out_shape=(
            jax.ShapeDtypeStruct((width, latents), jnp.float32),
            jax.ShapeDtypeStruct((1, latents), jnp.float32),
        ),
        in_specs=[pl.BlockSpec((rows, block), lambda i: (0, i))]
        + [pl.BlockSpec((part, latents), lambda i: (0, 0))] * parts,
        out_specs=(
            pl.BlockSpec((block, latents), lambda i: (i, 0)),
            pl.BlockSpec((1, latents), lambda i: (0, 0)),
        ),
        compiler_params=PARAMS,
        cost_estimate=pl.CostEstimate(
            flops=2 * rows * latents * width,
            bytes_accessed=latents * width * 4,
            transcendentals=0,
        ),
    )(acts, *deltas)


def make_per_device(n_layer, n_latent):
    depth = n_latent // LOCAL

    def swap(array, bit):
        return lax.ppermute(array, "latent", [(i, i ^ bit) for i in range(n_latent)])

    def shift(array, step):
        pairs = [(i, (i + step * LOCAL) % n_latent) for i in range(n_latent)]
        return lax.ppermute(array, "latent", pairs)

    def other_layer(array):
        return lax.ppermute(array, "layer", [(0, 1), (1, 0)])

    def over_layer(array, other):
        own = array.astype(jnp.float32)
        if n_layer == 2:
            return own + other.astype(jnp.float32)
        return lax.psum(own, "layer")

    groups = [[z * LOCAL + c for z in range(depth)] for c in range(LOCAL)]

    def per_device(acts, enc_weight, enc_bias, dec_weight, dec_bias):
        rows = acts.shape[0]
        parts = split_rows(rows)
        part = rows // parts
        scale = 1.0 / jnp.sqrt(jnp.float32(rows))
        sparsity = 1.0
        index = lax.axis_index("latent")
        z, x, core = index // LOCAL, (index // 2) % 2, index % 2

        done = []

        def send_layer(array):
            if n_layer != 2:
                return array, None
            if len(done) >= 2:
                array, earlier = lax.optimization_barrier((array, done[-2]))
                del earlier
            other = other_layer(array)
            done.append(other)
            return array, other

        dec_f = dec_weight.astype(jnp.float32)
        squares = jnp.sum(dec_f * dec_f, axis=1)
        squares = over_layer(squares, other_layer(squares) if n_layer == 2 else None)
        norms = jnp.sqrt(squares + 1e-06)

        def encode(k):
            block = acts[k * part : (k + 1) * part]
            own = jnp.dot(block, enc_weight, preferred_element_type=jnp.float32)
            return send_layer(own.astype(jnp.float16))

        def reduce_latent(partial):
            half, quarter = part // 2, part // 4
            piece = quarter // depth
            got = swap(rows_of(partial, (1 - core) * half, half), 1)
            held = rows_of(partial, core * half, half) + got
            got = swap(rows_of(held, (1 - x) * quarter, quarter).astype(jnp.bfloat16), 2)
            held = rows_of(held, x * quarter, quarter) + got.astype(jnp.float32)
            if depth > 4:
                return lax.psum_scatter(
                    held, "latent", scatter_dimension=0, axis_index_groups=groups, tiled=True
                )
            total = rows_of(held, z * piece, piece)
            for step in range(1, depth):
                target = (z + step) % depth
                got = shift(rows_of(held, target * piece, piece).astype(jnp.bfloat16), step)
                total = total + got.astype(jnp.float32)
            return total

        def gather_latent(own):
            piece = own.shape[0]
            if depth > 4:
                held = lax.all_gather(own, "latent", axis_index_groups=groups, tiled=True)
            else:
                held = jnp.zeros((piece * depth, own.shape[1]), own.dtype)
                held = lax.dynamic_update_slice_in_dim(held, own, z * piece, axis=0)
                for step in range(1, depth):
                    source = (z - step + depth) % depth
                    held = lax.dynamic_update_slice_in_dim(
                        held, shift(own, step), source * piece, axis=0
                    )
            for bit, place in ((2, x), (1, core)):
                got = swap(held, bit)
                low = jnp.where(place == 0, held, got)
                high = jnp.where(place == 0, got, held)
                held = jnp.concatenate([low, high], axis=0)
            return held

        def decode(k, own, other):
            pre = over_layer(own, other) + enc_bias
            codes = jax.nn.softplus(pre).astype(jnp.bfloat16)
            partial = jnp.dot(codes, dec_weight, preferred_element_type=jnp.float32)
            total = reduce_latent(partial)
            piece = total.shape[0]
            start = k * part + core * (part // 2) + x * (part // 4) + z * piece
            mine = rows_of(acts, start, piece).astype(jnp.float32)
            err = (2.0 * scale * (total + dec_bias - mine)).astype(jnp.bfloat16)
            return codes, gather_latent(err)

        def back_of(err):
            own = lax.dot_general(
                err, dec_weight, (((1,), (1,)), ((), ())), preferred_element_type=jnp.float32
            )
            return send_layer(own.astype(jnp.bfloat16))

        pres = [encode(k) for k in range(parts)]
        codes, errs = [], []
        for k in range(parts):
            own, other = pres[k]
            if k >= 2:
                own, earlier = lax.optimization_barrier((own, errs[k - 2]))
                del earlier
            c, e = decode(k, own, other)
            codes.append(c)
            errs.append(e)
        backs = [back_of(e) for e in errs]

        column = sum(jnp.sum(c.astype(jnp.float32), axis=0) for c in codes)
        grad_dec_bias = sum(jnp.sum(e.astype(jnp.float32), axis=0) for e in errs)
        coef = (sparsity * scale * column / norms)[:, None]
        grad_dec = grad_dec_of(codes, errs, coef, dec_weight)

        deltas = []
        for k in range(parts):
            slope = jax.nn.sigmoid(over_layer(*pres[k]) + enc_bias)
            own, other = backs[k]
            if k == parts - 1 and n_layer == 2:
                other, earlier = lax.optimization_barrier((other, grad_dec))
                del earlier
            back = over_layer(own, other) + sparsity * scale * norms
            deltas.append((back * slope).astype(jnp.bfloat16))
        grad_enc, grad_enc_bias = grad_enc_of(acts, deltas)
        return (grad_enc, grad_enc_bias[0], grad_dec, grad_dec_bias)

    return per_device


def solution(mesh):
    return jax.shard_map(
        make_per_device(mesh.shape["layer"], mesh.shape["latent"]),
        mesh=mesh,
        in_specs=(
            P(None, "layer"),
            P("layer", "latent"),
            P("latent"),
            P("latent", "layer"),
            P("layer"),
        ),
        out_specs=(P("layer", "latent"), P("latent"), P("latent", "layer"), P("layer")),
        check_vma=False,
    )
```
